32 devices in a mesh: dp: 16 (over z, y, core), mp: 2 (over x).
Axes of the slice: x: 2, y: 2, z: 4, core: 2. Of those that a mesh axis runs over, the one named last changes fastest.
Arguments:
- tiles: bfloat16 [8192, 1152], P('dp'), may hold values from -6 to 6
- norm_gain: float32 [1152], replicated, may hold values from 0.1 to 1.9
- norm_bias: float32 [1152], replicated, may hold values from -3 to 3
- expand_weight: bfloat16 [1152, 4304], P(None, 'mp'), may hold values from -0.1875 to 0.1875
- reduce_weight: bfloat16 [4304, 1152], P('mp'), may hold values from -0.09375 to 0.09375
- projector: bfloat16 [1152, 8192], P(None, 'mp'), may hold values from -0.1875 to 0.1875
- projector_bias: float32 [8192], P('mp'), may hold values from -3 to 3
- tile_counts: int32 [16, 2], replicated, may hold values from 1 to 9, as said below
- tile_owner: int32 [16, 16], replicated, may hold values from 0 to 15, as said below
- tile_slot: int32 [16, 16], replicated, may hold values from 0 to 15, as said below
- segment_ids: int32 [16, 640], P('dp'), may hold values from 0 to 3, never falling along the last dimension, each value on 1 to 320 neighbouring positions
- text_embed: bfloat16 [10240, 8192], P('dp', 'mp'), may hold values from -6 to 6
- input_gain: float32 [8192], replicated, may hold values from 0.6 to 8
- q_weight: bfloat16 [8192, 4096], P('dp', 'mp'), may hold values from -0.044194174 to 0.044194174
- k_weight: bfloat16 [8192, 1024], P('dp', 'mp'), may hold values from -0.044194174 to 0.044194174
- v_weight: bfloat16 [8192, 1024], P('dp', 'mp'), may hold values from -0.0625 to 0.0625
- feature_grad: bfloat16 [8192, 1152], P('dp'), may hold values from -6 to 6
Outputs:
- context: bfloat16 [10240, 4096], P('dp', 'mp')
- expand_grad: float32 [1152, 4304], P('dp', 'mp')
- reduce_grad_t: float32 [1152, 4304], P('dp', 'mp')
The draws below stay inside these ranges and needn't reach their ends.
Inputs may be any that keep to these rules, and one draw needn't show every extreme that they name: `tile_counts`: each index of dp has two images, together at most 16 tiles; some index has exactly 16, some image has 9. `tile_owner`: the tile slots of one index of dp name distinct owners; every owner is named by exactly 16 tile slots in all, at most one of each index. `tile_slot`: the tile slots that name one owner name distinct image slots.
All inputs are finite; a program needn't handle non-finite values.
Results may differ from the reference program's by a relative error of at most 0.011.
Values may be sent and summed in bfloat16 or wider, within the bound.
A program may use at most 256 MiB of HBM per device.

```python
import math
import jax
import jax.numpy as jnp
import numpy as np
from jax import lax

D_E = 1152
FF_E = 4304
D = 8192
HEAD = 128
KVHEADS = 8
QHEADS = 32
TILE_CAP = 16
TILE_ROWS = 32
ENC_ROWS = 512
MB_ROWS = 640
ROWS_E = 8192
ROWS = 10240
N_DP = 16


def routing_tables(key):
    key = jax.random.fold_in(key, 77)
    shift_key, slot_key = jax.random.split(key)
    shift = jax.random.permutation(shift_key, N_DP)[:TILE_CAP].astype(jnp.int32)
    owners = (jnp.arange(N_DP, dtype=jnp.int32)[:, None] + shift[None, :]) % N_DP
    orders = jax.vmap(lambda subkey: jax.random.permutation(subkey, TILE_CAP))(jax.random.split(slot_key, N_DP)).astype(jnp.int32)
    slots = orders[owners, jnp.arange(TILE_CAP, dtype=jnp.int32)[None, :]]
    return (owners.astype(jnp.int32), slots.astype(jnp.int32))


def draw_tile_counts(key, part):
    key = jax.random.fold_in(key, 1)
    first_key, second_key, chosen_key = jax.random.split(key, 3)
    first = jax.random.randint(first_key, (N_DP,), 1, 10)
    room = jnp.minimum(9, TILE_CAP - first)
    second = jax.random.randint(second_key, (N_DP,), 0, 1048576) % room + 1
    chosen = jax.random.randint(chosen_key, (), 0, N_DP)
    marks = jnp.arange(N_DP) == chosen
    first = jnp.where(marks, 9, first)
    second = jnp.where(marks, TILE_CAP - 9, second)
    return jnp.stack([first, second], axis=1).astype(jnp.int32)


def draw_tile_owner(key, part):
    owners, slots = routing_tables(key)
    return owners


def draw_tile_slot(key, part):
    owners, slots = routing_tables(key)
    return slots


def draw_input_gain(key, part):
    key = jax.random.fold_in(key, 3)
    logs = jax.random.uniform(key, (D,), jnp.float32, jnp.log(0.6), jnp.log(1.6))
    return jnp.exp(logs).astype(jnp.float32)


def draw_q_weight(key, part):
    key = jax.random.fold_in(key, 4)
    noise = jax.random.normal(key, (D, QHEADS, HEAD), jnp.float32)
    mixed = noise
    return (jnp.clip(mixed, -4.0, 4.0) * D ** (-0.5)).reshape(D, QHEADS * HEAD).astype(jnp.bfloat16)


def draw_k_weight(key, part):
    key = jax.random.fold_in(key, 5)
    noise = jax.random.normal(key, (D, KVHEADS, HEAD), jnp.float32)
    mixed = noise
    return (jnp.clip(mixed, -4.0, 4.0) * D ** (-0.5)).reshape(D, KVHEADS * HEAD).astype(jnp.bfloat16)


def with_spikes(entries, rng, source, target, shards_of, factor):
    owner, partner = [(jnp.arange(entries.shape[axis_at]) // (entries.shape[axis_at] // shards_of)).reshape([-1 if axis == axis_at else 1 for axis in range(entries.ndim)]) for axis_at in (source, target)]
    chosen = jax.random.permutation(rng, shards_of)[partner]
    strong = (owner == chosen) | (owner == (partner + shards_of // 2) % shards_of)
    return jnp.where(strong, factor * entries, entries)


def level_of(stream_key, shape, pieces, low, high):
    loudness, own = 1.0, jax.random.fold_in(stream_key, 6)
    for position, blocks in pieces:
        heights = jnp.exp(jax.random.uniform(jax.random.fold_in(own, position), (blocks,), jnp.float32, low / len(pieces), high / len(pieces)))
        loudness = loudness * jnp.repeat(heights, shape[position] // blocks).reshape([-1 if axis == position else 1 for axis in range(len(shape))])
    return loudness


def split_up(amount, total, bound, slope):
    loads = [(1 << 20) // math.isqrt(standing ** slope) + 1 for standing in range(2, amount + 1)]
    spare, holding = total - bound - (amount - 1), [1] * (amount - 1)
    while spare > 0:
        free = [i for i in range(amount - 1) if holding[i] < bound]
        pool, left = sum([loads[i] for i in free]), spare
        for i in free:
            extra = min(bound - holding[i], max(1, left * loads[i] // pool), spare)
            holding[i] = holding[i] + extra
            spare = spare - extra
    return np.array([bound] + holding)


def uneven_parts(own_key, number_of, total, limit, slope):
    if number_of == 2:
        one = jax.random.randint(own_key, (), max(1, total - limit), min(limit, total - 1) + 1)
        return jnp.stack([one, total - one])
    tallies = jnp.asarray(split_up(number_of, total, limit, slope), jnp.int32)
    pairs = (number_of - 1) // 2
    source_of, receiver = tallies[1:1 + 2 * pairs:2], tallies[2:2 + 2 * pairs:2]
    margin = jnp.minimum(source_of - 1, limit - receiver)
    moved = jax.random.randint(jax.random.fold_in(own_key, 1), (pairs,), 0, 1 << 20) % (margin + 1)
    tallies = tallies.at[1:1 + 2 * pairs:2].set(source_of - moved).at[2:2 + 2 * pairs:2].set(receiver + moved)
    return tallies[jax.random.permutation(jax.random.fold_in(own_key, 2), number_of)]


def centred(key, extent, scale, most, cuts=(), kind=jnp.bfloat16):
    result = scale * jax.random.normal(key, extent, jnp.float32)
    if cuts:
        result = result * level_of(key, extent, cuts, -0.22, 0.18)
    return jnp.clip(result, -most, most).astype(kind)


def bell_draw_with(rng, dims, deviation, bound, pieces, heavy, kind=jnp.bfloat16):
    entries = deviation * jax.random.normal(rng, dims, jnp.float32)
    if pieces:
        entries = entries * level_of(rng, dims, pieces, -0.22, 0.18)
    return jnp.clip(with_spikes(entries, jax.random.fold_in(rng, 3), *heavy), -bound, bound).astype(kind)


def setup_inputs(seed: int = 0) -> dict:
    arg_keys = jax.random.split(jax.random.key(seed), 18)
    tiles = bell_draw_with(arg_keys[0], (ROWS_E, D_E), 1.0, 6.0, ((0, 16),), (0, 1, 16, 2.0))
    norm_gain = jnp.clip(1.0 + 0.18 * jax.random.normal(arg_keys[1], (D_E,), jnp.float32), 0.1, 1.9)
    norm_bias = centred(arg_keys[2], (D_E,), 0.5, 3.0, (), jnp.float32)
    expand_weight = centred(arg_keys[3], (D_E, FF_E), D_E ** -0.5, 0.1875, ((1, 2),))
    reduce_weight = centred(arg_keys[4], (FF_E, D_E), FF_E ** -0.5, 0.09375, ((0, 2),))
    projector = centred(arg_keys[5], (D_E, D), D_E ** -0.5, 0.1875, ((1, 2),))
    projector_bias = centred(arg_keys[6], (D,), 0.5, 3.0, ((0, 2),), jnp.float32)
    tile_counts = draw_tile_counts(jax.random.fold_in(arg_keys[17], 71), 0)
    tile_owner = draw_tile_owner(jax.random.fold_in(arg_keys[17], 71), 0)
    tile_slot = draw_tile_slot(jax.random.fold_in(arg_keys[17], 71), 0)
    segment_ids = jax.vmap(lambda own: jnp.searchsorted(jnp.cumsum(uneven_parts(own, 4, MB_ROWS, MB_ROWS // 2, 2)), jnp.arange(MB_ROWS), side="right"))(jax.random.split(arg_keys[10], N_DP)).reshape((N_DP, MB_ROWS)).astype(jnp.int32)
    text_embed = centred(arg_keys[11], (ROWS, D), 1.0, 6.0, ((0, 16), (1, 2)))
    input_gain = draw_input_gain(jax.random.fold_in(arg_keys[17], 71), 0)
    q_weight = draw_q_weight(jax.random.fold_in(arg_keys[17], 71), 0)
    k_weight = draw_k_weight(jax.random.fold_in(arg_keys[17], 71), 0)
    v_weight = centred(arg_keys[15], (D, KVHEADS * HEAD), D ** -0.5, 0.0625, ((0, 16), (1, 2)))
    feature_grad = bell_draw_with(arg_keys[16], (ROWS_E, D_E), 1.0, 6.0, ((0, 16),), (0, 1, 16, 2.0))
    return dict(tiles=tiles, norm_gain=norm_gain, norm_bias=norm_bias, expand_weight=expand_weight, reduce_weight=reduce_weight, projector=projector, projector_bias=projector_bias, tile_counts=tile_counts, tile_owner=tile_owner, tile_slot=tile_slot, segment_ids=segment_ids, text_embed=text_embed, input_gain=input_gain, q_weight=q_weight, k_weight=k_weight, v_weight=v_weight, feature_grad=feature_grad)


def encoder_front(tiles, norm_gain, norm_bias, expand_weight):
    values = tiles.astype(jnp.float32)
    center = values - lax.optimization_barrier(jnp.mean(values, axis=1, keepdims=True))
    variance = lax.optimization_barrier(jnp.mean(center * center, axis=1, keepdims=True))
    normed = (center * lax.rsqrt(variance + 1e-06) * norm_gain + norm_bias).astype(jnp.bfloat16)
    pre_act = jnp.dot(normed, expand_weight, preferred_element_type=jnp.float32)
    hidden_units = jax.nn.gelu(pre_act, approximate=True).astype(jnp.bfloat16)
    return (normed, pre_act, hidden_units)

def gelu_slope(pre_act):
    factor = math.sqrt(2.0 / math.pi)
    inner = factor * (pre_act + 0.044715 * pre_act ** 3)
    tangent = jnp.tanh(inner)
    return 0.5 * (1.0 + tangent) + 0.5 * pre_act * (1.0 - tangent * tangent) * factor * (1.0 + 3.0 * 0.044715 * pre_act * pre_act)

def segment_positions(segments):
    count = segments.shape[0]
    index = jnp.arange(count, dtype=jnp.int32)
    same = segments[:, None] == segments[None, :]
    first = lax.optimization_barrier(jnp.min(jnp.where(same, index[None, :], count), axis=1))
    return index - first

def rotate(values, positions):
    width = values.shape[-1]
    half = width // 2
    freq = 1000000.0 ** (-(jnp.arange(half, dtype=jnp.float32) * 2.0 / width))
    angle = positions.astype(jnp.float32)[:, None] * freq[None, :]
    cosine = jnp.concatenate([jnp.cos(angle), jnp.cos(angle)], axis=1)[:, None, :]
    sine = jnp.concatenate([jnp.sin(angle), jnp.sin(angle)], axis=1)[:, None, :]
    turned = jnp.concatenate([-values[..., half:], values[..., :half]], axis=-1)
    return values * cosine + turned * sine

def attend(queries, keys, values, segments):
    count = queries.shape[0]
    kv_heads = keys.shape[1]
    grouped = queries.reshape(count, kv_heads, queries.shape[1] // kv_heads, queries.shape[2])
    scores = jnp.einsum('qgrd,kgd->grqk', grouped.astype(jnp.float32), keys.astype(jnp.float32)) * (1.0 / math.sqrt(queries.shape[2]))
    index = jnp.arange(count, dtype=jnp.int32)
    allowed = (index[None, :] <= index[:, None]) & (segments[None, :] == segments[:, None])
    scores = jnp.where(allowed[None, None], scores, -1e+30)
    top = lax.optimization_barrier(jnp.max(scores, axis=-1, keepdims=True))
    weights = jnp.exp(scores - top)
    probs = (weights / lax.optimization_barrier(jnp.sum(weights, axis=-1, keepdims=True))).astype(jnp.bfloat16)
    context = jnp.einsum('grqk,kgd->qgrd', probs.astype(jnp.float32), values.astype(jnp.float32))
    return context.reshape(count, -1).astype(jnp.bfloat16)

def reference(tiles, norm_gain, norm_bias, expand_weight, reduce_weight, projector, projector_bias, tile_counts, tile_owner, tile_slot, segment_ids, text_embed, input_gain, q_weight, k_weight, v_weight, feature_grad):
    normed, pre_act, hidden_units = encoder_front(tiles, norm_gain, norm_bias, expand_weight)
    enc_out = (tiles.astype(jnp.float32) + jnp.dot(hidden_units, reduce_weight, preferred_element_type=jnp.float32)).astype(jnp.bfloat16)
    projected = (jnp.dot(enc_out, projector, preferred_element_type=jnp.float32) + projector_bias).astype(jnp.bfloat16)
    tile_blocks = projected.reshape(N_DP * TILE_CAP, TILE_ROWS, D)
    totals = lax.optimization_barrier(jnp.sum(tile_counts, axis=1))
    live = jnp.arange(TILE_CAP, dtype=jnp.int32)[None, :] < totals[:, None]
    live_flat = live.reshape(-1)
    owner_flat = tile_owner.reshape(-1)
    slot_flat = tile_slot.reshape(-1)
    tile_index = jnp.arange(N_DP * TILE_CAP, dtype=jnp.int32)
    slot_index = jnp.arange(TILE_CAP, dtype=jnp.int32)
    texts = text_embed.reshape(N_DP, MB_ROWS, D)

    def one_owner(inputs):
        owner, segments, text_rows = inputs
        match = (live_flat & (owner_flat == owner))[None, :] & (slot_flat[None, :] == slot_index[:, None])
        filled = lax.optimization_barrier(jnp.sum(match.astype(jnp.int32), axis=1))
        source = lax.optimization_barrier(jnp.sum(jnp.where(match, tile_index[None, :], 0), axis=1)).astype(jnp.int32)
        images = tile_blocks[source]
        head_text = text_rows[:ENC_ROWS].reshape(TILE_CAP, TILE_ROWS, D)
        front = jnp.where(filled[:, None, None] > 0, images, head_text).reshape(ENC_ROWS, D)
        stream = jnp.concatenate([front, text_rows[ENC_ROWS:]], axis=0)
        row_values = stream.astype(jnp.float32)
        inverse = lax.rsqrt(lax.optimization_barrier(jnp.mean(row_values * row_values, axis=1)) + 1e-06)[:, None]
        scaled = (row_values * input_gain).astype(jnp.bfloat16)
        positions = segment_positions(segments)
        queries = (jnp.dot(scaled, q_weight, preferred_element_type=jnp.float32) * inverse).reshape(MB_ROWS, QHEADS, HEAD)
        keys = (jnp.dot(scaled, k_weight, preferred_element_type=jnp.float32) * inverse).reshape(MB_ROWS, KVHEADS, HEAD)
        values = (jnp.dot(scaled, v_weight, preferred_element_type=jnp.float32) * inverse).reshape(MB_ROWS, KVHEADS, HEAD)
        queries = rotate(queries, positions).astype(jnp.bfloat16)
        keys = rotate(keys, positions).astype(jnp.bfloat16)
        return attend(queries, keys, values.astype(jnp.bfloat16), segments)
    context = lax.map(one_owner, (jnp.arange(N_DP, dtype=jnp.int32), segment_ids, texts))
    context = context.reshape(ROWS, QHEADS * HEAD)
    live_rows = jnp.repeat(live_flat, TILE_ROWS)[:, None]
    cotangent = jnp.where(live_rows, feature_grad, jnp.zeros_like(feature_grad))
    reduce_grad_t = jnp.dot(cotangent.T, hidden_units, preferred_element_type=jnp.float32)
    hidden_grad = jnp.dot(cotangent, reduce_weight.T, preferred_element_type=jnp.float32)
    act_grad = (hidden_grad * gelu_slope(pre_act)).astype(jnp.bfloat16)
    expand_grad = jnp.dot(normed.T, act_grad, preferred_element_type=jnp.float32)
    return (context, expand_grad, reduce_grad_t)
```

```python
import math

import jax
import jax.numpy as jnp
from jax import lax
from jax.experimental import pallas as pl
from jax.experimental.pallas import tpu as pltpu
from jax.sharding import PartitionSpec as P

D = 8192
HEAD = 128
TILE_ROWS = 32


def encoder_front(tiles, norm_gain, norm_bias, expand_weight):
    values = tiles.astype(jnp.float32)
    center = values - jnp.mean(values, axis=1, keepdims=True)
    variance = jnp.mean(center * center, axis=1, keepdims=True)
    normed = (center * lax.rsqrt(variance + 1e-06) * norm_gain + norm_bias).astype(jnp.bfloat16)
    pre_act = jnp.dot(normed, expand_weight, preferred_element_type=jnp.float32)
    hidden_units = jax.nn.gelu(pre_act, approximate=True).astype(jnp.bfloat16)
    return (normed, pre_act, hidden_units)


def gelu_slope(pre_act):
    factor = math.sqrt(2.0 / math.pi)
    inner = factor * (pre_act + 0.044715 * pre_act**3)
    tangent = jnp.tanh(inner)
    return 0.5 * (1.0 + tangent) + 0.5 * pre_act * (1.0 - tangent * tangent) * factor * (
        1.0 + 3.0 * 0.044715 * pre_act * pre_act
    )


def segment_positions(segments):
    count = segments.shape[0]
    index = jnp.arange(count, dtype=jnp.int32)
    same = segments[:, None] == segments[None, :]
    first = jnp.min(jnp.where(same, index[None, :], count), axis=1)
    return index - first


def rope_tables(positions):
    half = HEAD // 2
    freq = 1000000.0 ** (-(jnp.arange(half, dtype=jnp.float32) * 2.0 / HEAD))
    angle = positions.astype(jnp.float32)[:, None] * freq[None, :]
    cosine, sine = jnp.cos(angle), jnp.sin(angle)
    return (
        jnp.concatenate([cosine, cosine], axis=1),
        jnp.concatenate([-sine, sine], axis=1),
    )


def attention_kernel(q_ref, k_ref, v_ref, inv_ref, cos_ref, sin_ref, row_ref, col_ref, out_ref):
    count = q_ref.shape[0]
    inverse = inv_ref[...]
    cosine = cos_ref[...]
    sine = sin_ref[...]

    def turn(raw):
        raw = raw * inverse
        return (raw * cosine + pltpu.roll(raw, HEAD // 2, 1) * sine).astype(jnp.bfloat16)

    keys = turn(k_ref[...])
    values = (v_ref[...] * inverse).astype(jnp.bfloat16)
    rows = lax.broadcasted_iota(jnp.int32, (count, count), 0)
    columns = lax.broadcasted_iota(jnp.int32, (count, count), 1)
    allowed = (columns <= rows) & (row_ref[...] == col_ref[...])
    for head in range(q_ref.shape[1] // HEAD):
        span = slice(head * HEAD, (head + 1) * HEAD)
        queries = turn(q_ref[:, span])
        scores = lax.dot_general(
            queries, keys, (((1,), (1,)), ((), ())), preferred_element_type=jnp.float32
        ) * (1.0 / math.sqrt(HEAD))
        scores = jnp.where(allowed, scores, -1e30)
        weights = jnp.exp(scores - jnp.max(scores, axis=1, keepdims=True))
        probs = (weights * (1.0 / jnp.sum(weights, axis=1, keepdims=True))).astype(jnp.bfloat16)
        out_ref[:, span] = jnp.dot(probs, values, preferred_element_type=jnp.float32).astype(
            jnp.bfloat16
        )


def attend(raw, q_cols, kv_cols, inverse, positions, segments):
    count = raw.shape[0]
    groups = kv_cols // HEAD
    wide = q_cols // groups
    cosine, sine = rope_tables(positions)
    q_blocks = q_cols // HEAD
    whole = lambda g: (0, 0)
    return pl.pallas_call(
        attention_kernel,
        grid=(groups,),
        in_specs=[
            pl.BlockSpec((count, wide), lambda g: (0, g)),
            pl.BlockSpec((count, HEAD), lambda g: (0, q_blocks + g)),
            pl.BlockSpec((count, HEAD), lambda g: (0, q_blocks + groups + g)),
            pl.BlockSpec((count, 1), whole),
            pl.BlockSpec((count, HEAD), whole),
            pl.BlockSpec((count, HEAD), whole),
            pl.BlockSpec((count, 1), whole),
            pl.BlockSpec((1, count), whole),
        ],
        out_specs=pl.BlockSpec((count, wide), lambda g: (0, g)),
        out_shape=jax.ShapeDtypeStruct((count, q_cols), jnp.bfloat16),
        compiler_params=pltpu.CompilerParams(vmem_limit_bytes=40 * 1024 * 1024),
        cost_estimate=pl.CostEstimate(
            flops=4 * count * count * q_cols,
            bytes_accessed=6 * count * q_cols,
            transcendentals=count * count * (q_cols // HEAD),
        ),
    )(
        raw, raw, raw, inverse[:, None], cosine, sine, segments[:, None], segments[None, :]
    )


def swap_mp(values):
    return lax.ppermute(values, "mp", [(0, 1), (1, 0)])


def sum_mp(partial):
    if lax.axis_size("mp") != 2:
        return lax.psum(partial, "mp")
    return partial + swap_mp(partial.astype(jnp.bfloat16)).astype(jnp.float32)


def gather_mp(top, tail):
    if lax.axis_size("mp") != 2:
        return lax.all_gather(jnp.concatenate([top, tail], axis=0), "mp", axis=1, tiled=True)
    other = jnp.concatenate([swap_mp(top), swap_mp(tail)], axis=0)
    own = jnp.concatenate([top, tail], axis=0)
    first = lax.axis_index("mp") == 0
    return jnp.concatenate(
        [jnp.where(first, own, other), jnp.where(first, other, own)], axis=1
    )


def sum_scatter(values):
    size = lax.axis_size("dp")
    me = lax.axis_index("dp")
    width = values.shape[1]
    rows = values.shape[0] // size
    total = values.reshape(size, rows, width)
    step = 1
    while step < size:
        pairs = total.reshape(total.shape[0] // 2, 2, rows, width)
        bit = (me // step) % 2
        mine = jnp.where(bit == 0, pairs[:, 0], pairs[:, 1])
        other = jnp.where(bit == 0, pairs[:, 1], pairs[:, 0]).astype(jnp.bfloat16)
        arrived = lax.ppermute(other, "dp", [(i, i ^ step) for i in range(size)])
        total = mine + arrived.astype(jnp.float32)
        step *= 2
    return total.reshape(rows, width)


def body(
    tiles,
    norm_gain,
    norm_bias,
    expand_weight,
    reduce_weight,
    projector,
    projector_bias,
    tile_counts,
    tile_owner,
    tile_slot,
    segment_ids,
    text_embed,
    input_gain,
    q_weight,
    k_weight,
    v_weight,
    feature_grad,
):
    group_size = lax.axis_size("dp")
    my_index = lax.axis_index("dp")
    slot_count = tile_owner.shape[1]
    tile_rows = TILE_ROWS
    enc_rows = tiles.shape[0]
    full_weights = lax.all_gather(
        jnp.concatenate([q_weight, k_weight, v_weight], axis=1), "dp", axis=0, tiled=True
    )
    totals = jnp.sum(tile_counts, axis=1)
    slot_ids = jnp.arange(slot_count, dtype=jnp.int32)
    live_all = slot_ids[None, :] < totals[:, None]
    my_live = lax.dynamic_index_in_dim(live_all, my_index, 0, keepdims=False)
    my_owner = lax.dynamic_index_in_dim(tile_owner, my_index, 0, keepdims=False)
    normed, pre_act, hidden_units = encoder_front(tiles, norm_gain, norm_bias, expand_weight)
    partial = jnp.dot(hidden_units, reduce_weight, preferred_element_type=jnp.float32)
    summed = sum_mp(partial)
    enc_out = (tiles.astype(jnp.float32) + summed).astype(jnp.bfloat16)
    outgoing = (
        (jnp.arange(group_size, dtype=jnp.int32)[:, None] == my_owner[None, :]) & my_live[None, :]
    ).astype(jnp.bfloat16)
    match = (tile_owner == my_index) & live_all
    filled = jnp.any(match, axis=1)
    slot_used = jnp.sum(jnp.where(match, tile_slot, 0), axis=1)
    placing = (filled[None, :] & (slot_used[None, :] == slot_ids[:, None])).astype(jnp.bfloat16)
    flat_tiles = enc_out.reshape(slot_count, -1)
    outbound = (
        jnp.dot(outgoing, flat_tiles, preferred_element_type=jnp.float32)
        .astype(jnp.bfloat16)
        .reshape(group_size, tile_rows, -1)
    )
    inbound = lax.all_to_all(outbound, "dp", split_axis=0, concat_axis=0, tiled=True)
    placed = (
        jnp.dot(placing, inbound.reshape(group_size, -1), preferred_element_type=jnp.float32)
        .astype(jnp.bfloat16)
        .reshape(enc_rows, -1)
    )
    images = (
        jnp.dot(placed, projector, preferred_element_type=jnp.float32) + projector_bias
    ).astype(jnp.bfloat16)
    is_image = jnp.repeat(jnp.sum(placing, axis=1) > 0, tile_rows)[:, None]
    top = jnp.where(is_image, images, text_embed[:enc_rows])
    piece_values = gather_mp(top, text_embed[enc_rows:]).astype(jnp.float32)
    scaled = (piece_values * input_gain).astype(jnp.bfloat16)
    squares = jnp.sum(piece_values * piece_values, axis=1)
    inverse = lax.rsqrt(squares / D + 1e-06)
    segments = segment_ids[0]
    positions = segment_positions(segments)
    scaled, inverse = lax.optimization_barrier((scaled, inverse))
    raw = jnp.dot(scaled, full_weights, preferred_element_type=jnp.float32)
    context = attend(raw, q_weight.shape[1], k_weight.shape[1], inverse, positions, segments)
    live_rows = jnp.repeat(my_live, tile_rows)[:, None]
    cotangent = jnp.where(live_rows, feature_grad, jnp.zeros_like(feature_grad))
    hidden_grad = lax.dot_general(
        cotangent, reduce_weight, (((1,), (1,)), ((), ())), preferred_element_type=jnp.float32
    )
    act_grad = (hidden_grad * gelu_slope(pre_act)).astype(jnp.bfloat16)
    reduce_grad_t = lax.dot_general(
        cotangent, hidden_units, (((0,), (0,)), ((), ())), preferred_element_type=jnp.float32
    )
    expand_grad = lax.dot_general(
        normed, act_grad, (((0,), (0,)), ((), ())), preferred_element_type=jnp.float32
    )
    expand_grad, reduce_grad_t = sum_scatter(expand_grad), sum_scatter(reduce_grad_t)
    return (context, expand_grad, reduce_grad_t)


def solution(mesh):
    in_specs = (
        P("dp", None),
        P(),
        P(),
        P(None, "mp"),
        P("mp", None),
        P(None, "mp"),
        P("mp"),
        P(),
        P(),
        P(),
        P("dp", None),
        P("dp", "mp"),
        P(),
        P("dp", "mp"),
        P("dp", "mp"),
        P("dp", "mp"),
        P("dp", None),
    )
    out_specs = (P("dp", "mp"), P("dp", "mp"), P("dp", "mp"))
    return jax.shard_map(body, mesh=mesh, in_specs=in_specs, out_specs=out_specs, check_vma=False)
```

```python
import math

import jax
import jax.numpy as jnp
from jax import lax
from jax.experimental import pallas as pl
from jax.experimental.pallas import tpu as pltpu
from jax.sharding import PartitionSpec as P

D = 8192
HEAD = 128
TILE_ROWS = 32


def encoder_front(tiles, norm_gain, norm_bias, expand_weight):
    values = tiles.astype(jnp.float32)
    center = values - jnp.mean(values, axis=1, keepdims=True)
    variance = jnp.mean(center * center, axis=1, keepdims=True)
    normed = (center * lax.rsqrt(variance + 1e-06) * norm_gain + norm_bias).astype(jnp.bfloat16)
    pre_act = jnp.dot(normed, expand_weight, preferred_element_type=jnp.float32)
    hidden_units = jax.nn.gelu(pre_act, approximate=True).astype(jnp.bfloat16)
    return (normed, pre_act, hidden_units)


def gelu_slope(pre_act):
    factor = math.sqrt(2.0 / math.pi)
    inner = factor * (pre_act + 0.044715 * pre_act**3)
    tangent = jnp.tanh(inner)
    return 0.5 * (1.0 + tangent) + 0.5 * pre_act * (1.0 - tangent * tangent) * factor * (
        1.0 + 3.0 * 0.044715 * pre_act * pre_act
    )


def segment_positions(segments):
    count = segments.shape[0]
    index = jnp.arange(count, dtype=jnp.int32)
    same = segments[:, None] == segments[None, :]
    first = jnp.min(jnp.where(same, index[None, :], count), axis=1)
    return index - first


def rope_tables(positions):
    half = HEAD // 2
    freq = 1000000.0 ** (-(jnp.arange(half, dtype=jnp.float32) * 2.0 / HEAD))
    angle = positions.astype(jnp.float32)[:, None] * freq[None, :]
    cosine, sine = jnp.cos(angle), jnp.sin(angle)
    return (
        jnp.concatenate([cosine, cosine], axis=1),
        jnp.concatenate([-sine, sine], axis=1),
    )


def attention_kernel(q_ref, k_ref, v_ref, inv_ref, cos_ref, sin_ref, row_ref, col_ref, out_ref):
    count = q_ref.shape[0]
    inverse = inv_ref[...]
    cosine = cos_ref[...]
    sine = sin_ref[...]

    def turn(raw):
        raw = raw * inverse
        return (raw * cosine + pltpu.roll(raw, HEAD // 2, 1) * sine).astype(jnp.bfloat16)

    keys = turn(k_ref[...])
    values = (v_ref[...] * inverse).astype(jnp.bfloat16)
    rows = lax.broadcasted_iota(jnp.int32, (count, count), 0)
    columns = lax.broadcasted_iota(jnp.int32, (count, count), 1)
    allowed = (columns <= rows) & (row_ref[...] == col_ref[...])
    for head in range(q_ref.shape[1] // HEAD):
        span = slice(head * HEAD, (head + 1) * HEAD)
        queries = turn(q_ref[:, span])
        scores = lax.dot_general(
            queries, keys, (((1,), (1,)), ((), ())), preferred_element_type=jnp.float32
        ) * (1.0 / math.sqrt(HEAD))
        scores = jnp.where(allowed, scores, -1e30)
        weights = jnp.exp(scores - jnp.max(scores, axis=1, keepdims=True))
        probs = (weights * (1.0 / jnp.sum(weights, axis=1, keepdims=True))).astype(jnp.bfloat16)
        out_ref[:, span] = jnp.dot(probs, values, preferred_element_type=jnp.float32).astype(
            jnp.bfloat16
        )


def attend(raw, q_cols, kv_cols, inverse, positions, segments):
    count = raw.shape[0]
    groups = kv_cols // HEAD
    wide = q_cols // groups
    cosine, sine = rope_tables(positions)
    q_blocks = q_cols // HEAD
    whole = lambda g: (0, 0)
    return pl.pallas_call(
        attention_kernel,
        grid=(groups,),
        in_specs=[
            pl.BlockSpec((count, wide), lambda g: (0, g)),
            pl.BlockSpec((count, HEAD), lambda g: (0, q_blocks + g)),
            pl.BlockSpec((count, HEAD), lambda g: (0, q_blocks + groups + g)),
            pl.BlockSpec((count, 1), whole),
            pl.BlockSpec((count, HEAD), whole),
            pl.BlockSpec((count, HEAD), whole),
            pl.BlockSpec((count, 1), whole),
            pl.BlockSpec((1, count), whole),
        ],
        out_specs=pl.BlockSpec((count, wide), lambda g: (0, g)),
        out_shape=jax.ShapeDtypeStruct((count, q_cols), jnp.bfloat16),
        compiler_params=pltpu.CompilerParams(vmem_limit_bytes=40 * 1024 * 1024),
        cost_estimate=pl.CostEstimate(
            flops=4 * count * count * q_cols,
            bytes_accessed=6 * count * q_cols,
            transcendentals=count * count * (q_cols // HEAD),
        ),
    )(
        raw, raw, raw, inverse[:, None], cosine, sine, segments[:, None], segments[None, :]
    )


def swap_mp(values):
    return lax.ppermute(values, "mp", [(0, 1), (1, 0)])


def sum_mp(partial):
    if lax.axis_size("mp") != 2:
        return lax.psum(partial, "mp")
    return partial + swap_mp(partial.astype(jnp.bfloat16)).astype(jnp.float32)


def gather_mp(top, tail):
    if lax.axis_size("mp") != 2:
        return lax.all_gather(jnp.concatenate([top, tail], axis=0), "mp", axis=1, tiled=True)
    other = jnp.concatenate([swap_mp(top), swap_mp(tail)], axis=0)
    own = jnp.concatenate([top, tail], axis=0)
    first = lax.axis_index("mp") == 0
    return jnp.concatenate(
        [jnp.where(first, own, other), jnp.where(first, other, own)], axis=1
    )


def sum_scatter(total, low, high):
    size = lax.axis_size("dp")
    me = lax.axis_index("dp")
    rows, width = total.shape[1:]
    step = low
    while step < high:
        pairs = total.reshape(total.shape[0] // 2, 2, rows, width)
        bit = (me // step) % 2
        mine = jnp.where(bit == 0, pairs[:, 0], pairs[:, 1])
        other = jnp.where(bit == 0, pairs[:, 1], pairs[:, 0]).astype(jnp.bfloat16)
        arrived = lax.ppermute(other, "dp", [(i, i ^ step) for i in range(size)])
        total = mine + arrived.astype(jnp.float32)
        step *= 2
    return total


def body(
    tiles,
    norm_gain,
    norm_bias,
    expand_weight,
    reduce_weight,
    projector,
    projector_bias,
    tile_counts,
    tile_owner,
    tile_slot,
    segment_ids,
    text_embed,
    input_gain,
    q_weight,
    k_weight,
    v_weight,
    feature_grad,
):
    group_size = lax.axis_size("dp")
    my_index = lax.axis_index("dp")
    slot_count = tile_owner.shape[1]
    tile_rows = TILE_ROWS
    enc_rows = tiles.shape[0]
    full_weights = lax.all_gather(
        jnp.concatenate([q_weight, k_weight, v_weight], axis=1), "dp", axis=0, tiled=True
    )
    totals = jnp.sum(tile_counts, axis=1)
    slot_ids = jnp.arange(slot_count, dtype=jnp.int32)
    live_all = slot_ids[None, :] < totals[:, None]
    my_live = lax.dynamic_index_in_dim(live_all, my_index, 0, keepdims=False)
    my_owner = lax.dynamic_index_in_dim(tile_owner, my_index, 0, keepdims=False)
    normed, pre_act, hidden_units = encoder_front(tiles, norm_gain, norm_bias, expand_weight)
    partial = jnp.dot(hidden_units, reduce_weight, preferred_element_type=jnp.float32)
    summed = sum_mp(partial)
    enc_out = (tiles.astype(jnp.float32) + summed).astype(jnp.bfloat16)
    outgoing = (
        (jnp.arange(group_size, dtype=jnp.int32)[:, None] == my_owner[None, :]) & my_live[None, :]
    ).astype(jnp.bfloat16)
    match = (tile_owner == my_index) & live_all
    filled = jnp.any(match, axis=1)
    slot_used = jnp.sum(jnp.where(match, tile_slot, 0), axis=1)
    placing = (filled[None, :] & (slot_used[None, :] == slot_ids[:, None])).astype(jnp.bfloat16)
    flat_tiles = enc_out.reshape(slot_count, -1)
    outbound = (
        jnp.dot(outgoing, flat_tiles, preferred_element_type=jnp.float32)
        .astype(jnp.bfloat16)
        .reshape(group_size, tile_rows, -1)
    )
    inbound = lax.all_to_all(outbound, "dp", split_axis=0, concat_axis=0, tiled=True)
    placed = (
        jnp.dot(placing, inbound.reshape(group_size, -1), preferred_element_type=jnp.float32)
        .astype(jnp.bfloat16)
        .reshape(enc_rows, -1)
    )
    images = (
        jnp.dot(placed, projector, preferred_element_type=jnp.float32) + projector_bias
    ).astype(jnp.bfloat16)
    is_image = jnp.repeat(jnp.sum(placing, axis=1) > 0, tile_rows)[:, None]
    top = jnp.where(is_image, images, text_embed[:enc_rows])
    piece_values = gather_mp(top, text_embed[enc_rows:]).astype(jnp.float32)
    scaled = (piece_values * input_gain).astype(jnp.bfloat16)
    squares = jnp.sum(piece_values * piece_values, axis=1)
    inverse = lax.rsqrt(squares / D + 1e-06)
    segments = segment_ids[0]
    positions = segment_positions(segments)
    live_rows = jnp.repeat(my_live, tile_rows)[:, None]
    cotangent = jnp.where(live_rows, feature_grad, jnp.zeros_like(feature_grad))
    hidden_grad = lax.dot_general(
        cotangent, reduce_weight, (((1,), (1,)), ((), ())), preferred_element_type=jnp.float32
    )
    act_grad = (hidden_grad * gelu_slope(pre_act)).astype(jnp.bfloat16)
    reduce_grad_t = lax.dot_general(
        cotangent, hidden_units, (((0,), (0,)), ((), ())), preferred_element_type=jnp.float32
    )
    expand_grad = lax.dot_general(
        normed, act_grad, (((0,), (0,)), ((), ())), preferred_element_type=jnp.float32
    )
    early = min(4, group_size)
    reduce_part, expand_part = (
        sum_scatter(grad.reshape(group_size, -1, grad.shape[1]), 1, early)
        for grad in (reduce_grad_t, expand_grad)
    )
    scaled, inverse, full_weights, reduce_part, expand_part = lax.optimization_barrier(
        (scaled, inverse, full_weights, reduce_part, expand_part)
    )
    raw = jnp.dot(scaled, full_weights, preferred_element_type=jnp.float32)
    context = attend(raw, q_weight.shape[1], k_weight.shape[1], inverse, positions, segments)
    reduce_grad_t, expand_grad = (
        sum_scatter(part, early, group_size)[0] for part in (reduce_part, expand_part)
    )
    return (context, expand_grad, reduce_grad_t)


def solution(mesh):
    in_specs = (
        P("dp", None),
        P(),
        P(),
        P(None, "mp"),
        P("mp", None),
        P(None, "mp"),
        P("mp"),
        P(),
        P(),
        P(),
        P("dp", None),
        P("dp", "mp"),
        P(),
        P("dp", "mp"),
        P("dp", "mp"),
        P("dp", "mp"),
        P("dp", None),
    )
    out_specs = (P("dp", "mp"), P("dp", "mp"), P("dp", "mp"))
    return jax.shard_map(body, mesh=mesh, in_specs=in_specs, out_specs=out_specs, check_vma=False)
```

```python
import math

import jax
import jax.numpy as jnp
from jax import lax
from jax.experimental import pallas as pl
from jax.experimental.pallas import tpu as pltpu
from jax.sharding import PartitionSpec as P

D = 8192
HEAD = 128
TILE_ROWS = 32


def encoder_front(tiles, norm_gain, norm_bias, expand_weight):
    values = tiles.astype(jnp.float32)
    center = values - jnp.mean(values, axis=1, keepdims=True)
    variance = jnp.mean(center * center, axis=1, keepdims=True)
    normed = (center * lax.rsqrt(variance + 1e-06) * norm_gain + norm_bias).astype(jnp.bfloat16)
    pre_act = jnp.dot(normed, expand_weight, preferred_element_type=jnp.float32)
    hidden_units = jax.nn.gelu(pre_act, approximate=True).astype(jnp.bfloat16)
    return (normed, pre_act, hidden_units)


def gelu_slope(pre_act):
    factor = math.sqrt(2.0 / math.pi)
    inner = factor * (pre_act + 0.044715 * pre_act**3)
    tangent = jnp.tanh(inner)
    return 0.5 * (1.0 + tangent) + 0.5 * pre_act * (1.0 - tangent * tangent) * factor * (
        1.0 + 3.0 * 0.044715 * pre_act * pre_act
    )


def segment_positions(segments):
    count = segments.shape[0]
    index = jnp.arange(count, dtype=jnp.int32)
    same = segments[:, None] == segments[None, :]
    first = jnp.min(jnp.where(same, index[None, :], count), axis=1)
    return index - first


def rope_tables(positions):
    half = HEAD // 2
    freq = 1000000.0 ** (-(jnp.arange(half, dtype=jnp.float32) * 2.0 / HEAD))
    angle = positions.astype(jnp.float32)[:, None] * freq[None, :]
    cosine, sine = jnp.cos(angle), jnp.sin(angle)
    return (
        jnp.concatenate([cosine, cosine], axis=1),
        jnp.concatenate([-sine, sine], axis=1),
    )


def attention_kernel(q_ref, k_ref, v_ref, inv_ref, cos_ref, sin_ref, row_ref, col_ref, out_ref):
    count = q_ref.shape[0]
    inverse = inv_ref[...]
    cosine = cos_ref[...]
    sine = sin_ref[...]

    def turn(raw):
        raw = raw * inverse
        return (raw * cosine + pltpu.roll(raw, HEAD // 2, 1) * sine).astype(jnp.bfloat16)

    keys = turn(k_ref[...])
    values = (v_ref[...] * inverse).astype(jnp.bfloat16)
    rows = lax.broadcasted_iota(jnp.int32, (count, count), 0)
    columns = lax.broadcasted_iota(jnp.int32, (count, count), 1)
    allowed = (columns <= rows) & (row_ref[...] == col_ref[...])
    for head in range(q_ref.shape[1] // HEAD):
        span = slice(head * HEAD, (head + 1) * HEAD)
        queries = turn(q_ref[:, span])
        scores = lax.dot_general(
            queries, keys, (((1,), (1,)), ((), ())), preferred_element_type=jnp.float32
        ) * (1.0 / math.sqrt(HEAD))
        scores = jnp.where(allowed, scores, -1e30)
        weights = jnp.exp(scores - jnp.max(scores, axis=1, keepdims=True))
        probs = (weights * (1.0 / jnp.sum(weights, axis=1, keepdims=True))).astype(jnp.bfloat16)
        out_ref[:, span] = jnp.dot(probs, values, preferred_element_type=jnp.float32).astype(
            jnp.bfloat16
        )


def attend(raw_q, raw_kv, q_cols, kv_cols, inverse, positions, segments):
    count = raw_q.shape[0]
    groups = kv_cols // HEAD
    wide = q_cols // groups
    cosine, sine = rope_tables(positions)
    whole = lambda g: (0, 0)
    return pl.pallas_call(
        attention_kernel,
        grid=(groups,),
        in_specs=[
            pl.BlockSpec((count, wide), lambda g: (0, g)),
            pl.BlockSpec((count, HEAD), lambda g: (0, g)),
            pl.BlockSpec((count, HEAD), lambda g: (0, groups + g)),
            pl.BlockSpec((count, 1), whole),
            pl.BlockSpec((count, HEAD), whole),
            pl.BlockSpec((count, HEAD), whole),
            pl.BlockSpec((count, 1), whole),
            pl.BlockSpec((1, count), whole),
        ],
        out_specs=pl.BlockSpec((count, wide), lambda g: (0, g)),
        out_shape=jax.ShapeDtypeStruct((count, q_cols), jnp.bfloat16),
        compiler_params=pltpu.CompilerParams(vmem_limit_bytes=40 * 1024 * 1024),
        cost_estimate=pl.CostEstimate(
            flops=4 * count * count * q_cols,
            bytes_accessed=6 * count * q_cols,
            transcendentals=count * count * (q_cols // HEAD),
        ),
    )(
        raw_q, raw_kv, raw_kv, inverse[:, None], cosine, sine, segments[:, None], segments[None, :]
    )


def swap_mp(values):
    return lax.ppermute(values, "mp", [(0, 1), (1, 0)])


def sum_mp(partial):
    if lax.axis_size("mp") != 2:
        return lax.psum(partial, "mp")
    return partial + swap_mp(partial.astype(jnp.bfloat16)).astype(jnp.float32)


def gather_mp(top, tail):
    if lax.axis_size("mp") != 2:
        return lax.all_gather(jnp.concatenate([top, tail], axis=0), "mp", axis=1, tiled=True)
    other = jnp.concatenate([swap_mp(top), swap_mp(tail)], axis=0)
    own = jnp.concatenate([top, tail], axis=0)
    first = lax.axis_index("mp") == 0
    return jnp.concatenate(
        [jnp.where(first, own, other), jnp.where(first, other, own)], axis=1
    )


def sum_scatter(values):
    size = lax.axis_size("dp")
    me = lax.axis_index("dp")
    width = values.shape[1]
    rows = values.shape[0] // size
    total = values.reshape(size, rows, width)
    step = 1
    while step < size:
        pairs = total.reshape(total.shape[0] // 2, 2, rows, width)
        bit = (me // step) % 2
        mine = jnp.where(bit == 0, pairs[:, 0], pairs[:, 1])
        other = jnp.where(bit == 0, pairs[:, 1], pairs[:, 0]).astype(jnp.bfloat16)
        arrived = lax.ppermute(other, "dp", [(i, i ^ step) for i in range(size)])
        total = mine + arrived.astype(jnp.float32)
        step *= 2
    return total.reshape(rows, width)


def body(
    tiles,
    norm_gain,
    norm_bias,
    expand_weight,
    reduce_weight,
    projector,
    projector_bias,
    tile_counts,
    tile_owner,
    tile_slot,
    segment_ids,
    text_embed,
    input_gain,
    q_weight,
    k_weight,
    v_weight,
    feature_grad,
):
    group_size = lax.axis_size("dp")
    my_index = lax.axis_index("dp")
    slot_count = tile_owner.shape[1]
    tile_rows = TILE_ROWS
    enc_rows = tiles.shape[0]
    full_q = lax.all_gather(q_weight, "dp", axis=0, tiled=True)
    full_kv = lax.all_gather(
        jnp.concatenate([k_weight, v_weight], axis=1), "dp", axis=0, tiled=True
    )
    totals = jnp.sum(tile_counts, axis=1)
    slot_ids = jnp.arange(slot_count, dtype=jnp.int32)
    live_all = slot_ids[None, :] < totals[:, None]
    my_live = lax.dynamic_index_in_dim(live_all, my_index, 0, keepdims=False)
    my_owner = lax.dynamic_index_in_dim(tile_owner, my_index, 0, keepdims=False)
    normed, pre_act, hidden_units = encoder_front(tiles, norm_gain, norm_bias, expand_weight)
    partial = jnp.dot(hidden_units, reduce_weight, preferred_element_type=jnp.float32)
    summed = sum_mp(partial)
    enc_out = (tiles.astype(jnp.float32) + summed).astype(jnp.bfloat16)
    outgoing = (
        (jnp.arange(group_size, dtype=jnp.int32)[:, None] == my_owner[None, :]) & my_live[None, :]
    ).astype(jnp.bfloat16)
    match = (tile_owner == my_index) & live_all
    filled = jnp.any(match, axis=1)
    slot_used = jnp.sum(jnp.where(match, tile_slot, 0), axis=1)
    placing = (filled[None, :] & (slot_used[None, :] == slot_ids[:, None])).astype(jnp.bfloat16)
    flat_tiles = enc_out.reshape(slot_count, -1)
    outbound = (
        jnp.dot(outgoing, flat_tiles, preferred_element_type=jnp.float32)
        .astype(jnp.bfloat16)
        .reshape(group_size, tile_rows, -1)
    )
    inbound = lax.all_to_all(outbound, "dp", split_axis=0, concat_axis=0, tiled=True)
    placed = (
        jnp.dot(placing, inbound.reshape(group_size, -1), preferred_element_type=jnp.float32)
        .astype(jnp.bfloat16)
        .reshape(enc_rows, -1)
    )
    images = (
        jnp.dot(placed, projector, preferred_element_type=jnp.float32) + projector_bias
    ).astype(jnp.bfloat16)
    is_image = jnp.repeat(jnp.sum(placing, axis=1) > 0, tile_rows)[:, None]
    top = jnp.where(is_image, images, text_embed[:enc_rows])
    piece_values = gather_mp(top, text_embed[enc_rows:]).astype(jnp.float32)
    scaled = (piece_values * input_gain).astype(jnp.bfloat16)
    squares = jnp.sum(piece_values * piece_values, axis=1)
    inverse = lax.rsqrt(squares / D + 1e-06)
    segments = segment_ids[0]
    positions = segment_positions(segments)
    scaled, inverse = lax.optimization_barrier((scaled, inverse))
    raw_q = jnp.dot(scaled, full_q, preferred_element_type=jnp.float32)
    raw_kv = jnp.dot(scaled, full_kv, preferred_element_type=jnp.float32)
    context = attend(raw_q, raw_kv, q_weight.shape[1], k_weight.shape[1], inverse, positions, segments)
    live_rows = jnp.repeat(my_live, tile_rows)[:, None]
    cotangent = jnp.where(live_rows, feature_grad, jnp.zeros_like(feature_grad))
    hidden_grad = lax.dot_general(
        cotangent, reduce_weight, (((1,), (1,)), ((), ())), preferred_element_type=jnp.float32
    )
    act_grad = (hidden_grad * gelu_slope(pre_act)).astype(jnp.bfloat16)
    reduce_grad_t = lax.dot_general(
        cotangent, hidden_units, (((0,), (0,)), ((), ())), preferred_element_type=jnp.float32
    )
    expand_grad = lax.dot_general(
        normed, act_grad, (((0,), (0,)), ((), ())), preferred_element_type=jnp.float32
    )
    expand_grad, reduce_grad_t = sum_scatter(expand_grad), sum_scatter(reduce_grad_t)
    return (context, expand_grad, reduce_grad_t)


def solution(mesh):
    in_specs = (
        P("dp", None),
        P(),
        P(),
        P(None, "mp"),
        P("mp", None),
        P(None, "mp"),
        P("mp"),
        P(),
        P(),
        P(),
        P("dp", None),
        P("dp", "mp"),
        P(),
        P("dp", "mp"),
        P("dp", "mp"),
        P("dp", "mp"),
        P("dp", None),
    )
    out_specs = (P("dp", "mp"), P("dp", "mp"), P("dp", "mp"))
    return jax.shard_map(body, mesh=mesh, in_specs=in_specs, out_specs=out_specs, check_vma=False)
```
